32 devices in a mesh: grid: 2 (over y), wide: 4 (over z), narrow: 4 (over x, core).
Axes of the slice: x: 2, y: 2, z: 4, core: 2. Of those that a mesh axis runs over, the one named last changes fastest.
Arguments:
- tokens: bfloat16 [4096, 8192], P(('grid', 'wide'), 'narrow'), parts along dimension 0, may hold values from -6 to 6
- frozen_value_weight: bfloat16 [8192, 1024], P('narrow'), may hold values from -0.0625 to 0.0625
- token_adapter_index: int32 [4096, 1], P(('grid', 'wide')), parts along dimension 0, may hold values from 0 to 7; in each aligned block of 512 rows (0 to 511, 512 to 1023, ...) at most 192 rows name the same one
- adapter_down_weight: float32 [16384, 128], P(('grid', 'narrow'), 'wide'), parts along dimension 0, may hold values from -0.0625 to 0.0625
- adapter_up_weight: float32 [256, 1024], P(('grid', 'wide'), 'narrow'), parts along dimension 0, may hold values from -0.1875 to 0.1875
- down_moment_first: float32 [16384, 128], P(('grid', 'narrow'), 'wide'), parts along dimension 0, may hold values from -12 to 12
- down_moment_second: float32 [16384, 128], P(('grid', 'narrow'), 'wide'), parts along dimension 0, may hold values from 1 to 100
- up_moment_first: float32 [256, 1024], P(('grid', 'wide'), 'narrow'), parts along dimension 0, may hold values from -12 to 12
- up_moment_second: float32 [256, 1024], P(('grid', 'wide'), 'narrow'), parts along dimension 0, may hold values from 1 to 100
- rates: float32 [16], P(('grid', 'wide')), parts along dimension 0, may hold values from 0.01 to 0.2
- value_output_gradient: bfloat16 [4096, 1024], P(('grid', 'wide', 'narrow')), parts along dimension 0, may hold values from -6 to 6
Outputs:
- values: bfloat16 [4096, 1024], P(('grid', 'wide', 'narrow')), parts along dimension 0
- grad_tokens: bfloat16 [4096, 8192], P(('grid', 'wide'), 'narrow'), parts along dimension 0
- updated_down_weight: float32 [16384, 128], P(('grid', 'narrow'), 'wide'), parts along dimension 0
- updated_down_moment_first: float32 [16384, 128], P(('grid', 'narrow'), 'wide'), parts along dimension 0
- updated_down_moment_second: float32 [16384, 128], P(('grid', 'narrow'), 'wide'), parts along dimension 0
- updated_up_weight: float32 [256, 1024], P(('grid', 'wide'), 'narrow'), parts along dimension 0
- updated_up_moment_first: float32 [256, 1024], P(('grid', 'wide'), 'narrow'), parts along dimension 0
- updated_up_moment_second: float32 [256, 1024], P(('grid', 'wide'), 'narrow'), parts along dimension 0
The draws below stay inside these ranges and needn't reach their ends.
There are 2 independent parts, one for each index of `grid`. The reference program is written for one: setup_inputs(seed, part) draws one part's arguments, and reference() takes and returns one part's arrays. A program takes and returns all parts, laid end to end along the dimension named above; an argument that names none is the same for every part. Nothing has to cross between parts.
Inputs may be any that keep to these rules, and one draw needn't show every extreme that they name: `token_adapter_index`: within the tokens of one index of wide (aligned blocks of 512 rows) no adapter is named by more than 192 rows, and in every draw some adapter is named by exactly 192 rows of some block.
All inputs are finite; a program needn't handle non-finite values.
Results may differ from the reference program's by a relative error of at most 0.009.
Values may be sent and summed in bfloat16 or wider, within the bound.
A program may use at most 64 MiB of HBM per device.

```python
import math
import jax
import jax.numpy as jnp
import numpy as np
from jax import lax

MODEL_WIDTH = 8192
VALUE_WIDTH = 1024
ADAPTER_RANK = 16
TOK_DEV = 512
STEP = 1000
ADAPTER_GRID = 8
TOKENS = 2048
CAP = 192


def block_scale(stream_key, shape, cuts, least, largest):
    def one(axis_at, shards_of):
        draws = jax.random.uniform(jax.random.fold_in(jax.random.fold_in(stream_key, 6), axis_at), (shards_of,), jnp.float32, least / len(cuts), largest / len(cuts))
        return jnp.repeat(jnp.exp(draws), shape[axis_at] // shards_of).reshape((-1,) + (1,) * (len(shape) - axis_at - 1))

    level = one(*cuts[0])
    for cut in cuts[1:]:
        level = level * one(*cut)
    return level


def shared_out(key, own, number, rows, count, top, reach, lean):
    order = jax.random.permutation(key, count)
    packed, ordinary = shares(count, rows * top, reach, lean, True), shares(count, rows * top, reach, lean, False)
    places = jnp.arange(count)

    def named(tallies, offset_by):
        used = int((tallies > 0).sum())
        fixed = max(1, used // 4)
        moved = fixed + (places - fixed + offset_by * (used - fixed)) % max(1, count - fixed)
        return jnp.zeros((count,), jnp.int32).at[order[jnp.where(places < fixed, places, moved)]].set(jnp.asarray(tallies, jnp.int32))

    tallies = jnp.where(number % 4 == 0, named(packed, number // 4), named(ordinary, number - number // 4 - 1))
    mixed = jax.random.permutation(jax.random.fold_in(own, 3), count)
    donor, sink = mixed[0:count // 2 * 2:2], mixed[1:count // 2 * 2:2]
    slack = jnp.minimum(tallies[donor] - 1, reach - tallies[sink]) // 2
    slack = jnp.where((donor == order[0]) | (sink == order[0]) | (tallies[sink] == 0), 0, jnp.maximum(slack, 0))
    moved = jax.random.randint(jax.random.fold_in(own, 4), (count // 2,), 0, 1 << 20) % (slack + 1)
    tallies = tallies.at[donor].add(-moved).at[sink].add(moved)
    labels = jnp.searchsorted(jnp.cumsum(tallies), jnp.arange(rows * top), side="right").astype(jnp.int32)
    table = labels.reshape(top, rows).T
    table = table[jax.random.permutation(jax.random.fold_in(own, 1), rows)]
    offset_by = jax.random.randint(jax.random.fold_in(own, 2), (rows, 1), 0, top)
    return jnp.take_along_axis(table, (jnp.arange(top)[None, :] + offset_by) % top, axis=1)


def shares(count, total, reach, skew, full):
    weights = [(1 << 20) // math.isqrt(rank ** skew) + 1 for rank in range(1, count + 1)]
    largest = reach if full else min(reach, max(-(-total // count), total * weights[0] // sum(weights)))
    least = 1 if total - largest >= count - 1 else 0
    counts, surplus = [largest] + [least] * (count - 1), total - largest - least * (count - 1)
    while surplus > 0:
        free = [i for i in range(1, count) if counts[i] < largest] or [i for i in range(1, count) if counts[i] < reach]
        mass, budget = sum([weights[i] for i in free]), surplus
        for i in free:
            extra = min(reach - counts[i], max(1, budget * weights[i] // mass), surplus)
            counts[i] = counts[i] + extra
            surplus = surplus - extra
    return np.array(counts)


def noise(stream_key, dims, width, limit, shards=(), kind=jnp.bfloat16):
    array = jax.random.normal(stream_key, dims, jnp.float32) * width
    if len(shards) > 0:
        array = block_scale(stream_key, dims, shards, -0.22, 0.18) * array
    return jnp.clip(array, min=-limit, max=limit).astype(kind)


def setup_inputs(seed: int = 0, part: int = 0) -> dict:
    key_list = jax.random.split(jax.random.key(seed), 12)
    own_keys = jax.random.split(jax.random.fold_in(key_list[11], part), 12)
    tokens = noise(own_keys[0], (TOKENS, MODEL_WIDTH), 1.0, 6.0, ((0, 4), (1, 4)))
    frozen_value_weight = noise(key_list[1], (MODEL_WIDTH, VALUE_WIDTH), MODEL_WIDTH ** -0.5, 0.0625, ((0, 4),))
    token_adapter_index_keys = jax.random.split(jax.random.fold_in(own_keys[2], 1), TOKENS // TOK_DEV)
    token_adapter_index_turns = jax.random.permutation(jax.random.fold_in(own_keys[2], 3), TOKENS // TOK_DEV)
    token_adapter_index = jax.vmap(lambda own, number: shared_out(jax.random.fold_in(own_keys[2], 2), own, number, TOK_DEV, ADAPTER_GRID, 1, CAP, 2))(token_adapter_index_keys, token_adapter_index_turns).reshape((TOKENS, 1))
    adapter_down_weight = noise(own_keys[3], (MODEL_WIDTH, ADAPTER_GRID * ADAPTER_RANK), MODEL_WIDTH ** -0.5, 0.0625, ((0, 4), (1, 4)), jnp.float32)
    adapter_up_weight = noise(own_keys[4], (ADAPTER_GRID * ADAPTER_RANK, VALUE_WIDTH), VALUE_WIDTH ** -0.5, 0.1875, ((0, 4), (1, 4)), jnp.float32)
    down_moment_first = noise(own_keys[5], (MODEL_WIDTH, ADAPTER_GRID * ADAPTER_RANK), 2.0, 12.0, ((0, 4), (1, 4)), jnp.float32)
    down_moment_second = jnp.clip(jnp.exp(math.log(100.0) - 4.6051702 * jax.random.uniform(own_keys[6], (MODEL_WIDTH, ADAPTER_GRID * ADAPTER_RANK), jnp.float32) ** block_scale(own_keys[6], (MODEL_WIDTH, ADAPTER_GRID * ADAPTER_RANK), ((0, 4), (1, 4)), -0.2, 0.2)), 1.0, 100.0)
    up_moment_first = noise(own_keys[7], (ADAPTER_GRID * ADAPTER_RANK, VALUE_WIDTH), 2.0, 12.0, ((0, 4), (1, 4)), jnp.float32)
    up_moment_second = jnp.clip(jnp.exp(math.log(100.0) - 4.6051702 * jax.random.uniform(own_keys[8], (ADAPTER_GRID * ADAPTER_RANK, VALUE_WIDTH), jnp.float32) ** block_scale(own_keys[8], (ADAPTER_GRID * ADAPTER_RANK, VALUE_WIDTH), ((0, 4), (1, 4)), -0.2, 0.2)), 1.0, 100.0)
    rates = jnp.clip(jnp.exp(math.log(0.2) - 2.9957323 * jax.random.uniform(own_keys[9], (ADAPTER_GRID,), jnp.float32) ** block_scale(own_keys[9], (ADAPTER_GRID,), ((0, 4),), -0.2, 0.2)), 0.01, 0.2)
    value_output_gradient = noise(own_keys[10], (TOKENS, VALUE_WIDTH), 1.0, 6.0, ((0, 16),))
    return dict(tokens=tokens, frozen_value_weight=frozen_value_weight, token_adapter_index=token_adapter_index, adapter_down_weight=adapter_down_weight, adapter_up_weight=adapter_up_weight, down_moment_first=down_moment_first, down_moment_second=down_moment_second, up_moment_first=up_moment_first, up_moment_second=up_moment_second, rates=rates, value_output_gradient=value_output_gradient)


adapter_scale = 2.0
beta_first = 0.9
beta_second = 0.999
adam_eps = 1e-08

def expand_codes(lowrank, selector):
    item_count = lowrank.shape[0]
    return (selector[:, :, None] * lowrank[:, None, :]).reshape(item_count, -1)

def packed_adapter_index(spread, selector):
    item_count = spread.shape[0]
    return lax.optimization_barrier(jnp.sum(spread.reshape(item_count, selector.shape[1], -1) * selector[:, :, None], axis=1))

def apply_adam_moments(parameter, first, second, gradient, step_rate):
    first_new = beta_first * first + (1.0 - beta_first) * gradient
    second_new = beta_second * second + (1.0 - beta_second) * gradient * gradient
    first_fix = 1.0 - beta_first ** STEP
    second_fix = 1.0 - beta_second ** STEP
    update = step_rate * (first_new / first_fix) / (jnp.sqrt(second_new / second_fix) + adam_eps)
    return (parameter - update, first_new, second_new)

def reference(tokens, frozen_value_weight, token_adapter_index, adapter_down_weight, adapter_up_weight, down_moment_first, down_moment_second, up_moment_first, up_moment_second, rates, value_output_gradient):
    adapter_members = adapter_down_weight.shape[1] // ADAPTER_RANK
    selector = token_adapter_index[:, 0:1] == jnp.arange(adapter_members, dtype=jnp.int32)[None, :]
    select_low = selector.astype(jnp.bfloat16)
    adapter_selector_full = selector.astype(jnp.float32)
    down_rank_rows = adapter_down_weight.astype(jnp.bfloat16)
    up_rank_rows = adapter_up_weight.astype(jnp.bfloat16)
    spread = jnp.dot(tokens, down_rank_rows, preferred_element_type=jnp.float32)
    code_low = packed_adapter_index(spread, adapter_selector_full).astype(jnp.bfloat16)
    wide_adapter_index = expand_codes(code_low, select_low)
    frozen_output = jnp.dot(tokens, frozen_value_weight, preferred_element_type=jnp.float32)
    rank_output_delta = jnp.dot(wide_adapter_index, up_rank_rows, preferred_element_type=jnp.float32)
    values = (frozen_output + adapter_scale * rank_output_delta).astype(jnp.bfloat16)
    returned_spread_rows = jnp.dot(value_output_gradient, up_rank_rows.T, preferred_element_type=jnp.float32)
    returned_rank_rows = (adapter_scale * packed_adapter_index(returned_spread_rows, adapter_selector_full)).astype(jnp.bfloat16)
    back_wide = expand_codes(returned_rank_rows, select_low)
    grad_tokens = (jnp.dot(value_output_gradient, frozen_value_weight.T, preferred_element_type=jnp.float32) + jnp.dot(back_wide, down_rank_rows.T, preferred_element_type=jnp.float32)).astype(jnp.bfloat16)
    down_weight_gradient = jnp.dot(tokens.T, back_wide, preferred_element_type=jnp.float32)
    up_weight_gradient = adapter_scale * jnp.dot(wide_adapter_index.T, value_output_gradient, preferred_element_type=jnp.float32)
    learning_rate_columns = jnp.repeat(rates, ADAPTER_RANK)
    updated_down_weight, updated_down_moment_first, updated_down_moment_second = apply_adam_moments(adapter_down_weight, down_moment_first, down_moment_second, down_weight_gradient, learning_rate_columns[None, :])
    updated_up_weight, updated_up_moment_first, updated_up_moment_second = apply_adam_moments(adapter_up_weight, up_moment_first, up_moment_second, up_weight_gradient, learning_rate_columns[:, None])
    return (values, grad_tokens, updated_down_weight, updated_down_moment_first, updated_down_moment_second, updated_up_weight, updated_up_moment_first, updated_up_moment_second)
```

```python
import functools

import jax
import jax.numpy as jnp
from jax import lax
from jax.experimental import pallas as pl
from jax.experimental.pallas import tpu as pltpu
from jax.sharding import PartitionSpec as P

ADAPTER_RANK = 16
STEP = 1000


adapter_scale = 2.0
beta_first = 0.9
beta_second = 0.999
adam_eps = 1e-08


def expand_codes(lowrank, selector):
    item_count = lowrank.shape[0]
    return (selector[:, :, None] * lowrank[:, None, :]).reshape(item_count, -1)


def packed_adapter_index(spread, selector):
    item_count = spread.shape[0]
    return jnp.sum(spread.reshape(item_count, selector.shape[1], -1) * selector[:, :, None], axis=1)


def apply_adam_moments(parameter, first, second, gradient, step_rate):
    first_new = beta_first * first + (1.0 - beta_first) * gradient
    second_new = beta_second * second + (1.0 - beta_second) * gradient * gradient
    first_fix = 1.0 - beta_first**STEP
    second_fix = 1.0 - beta_second**STEP
    update = step_rate * (first_new / first_fix) / (jnp.sqrt(second_new / second_fix) + adam_eps)
    return (parameter - update, first_new, second_new)


def shards(
    tokens,
    frozen_value_weight,
    token_adapter_index,
    adapter_down_weight,
    adapter_up_weight,
    down_moment_first,
    down_moment_second,
    up_moment_first,
    up_moment_second,
    rates,
    value_output_gradient,
):
    wide_adapter_count = lax.axis_size("wide")
    narrow_count = lax.axis_size("narrow")
    narrow_index = lax.axis_index("narrow")
    token_count = tokens.shape[0]
    row_count = token_count // narrow_count
    row_start = narrow_index * row_count
    adapter_members = adapter_down_weight.shape[1] * wide_adapter_count // ADAPTER_RANK
    selector = token_adapter_index == jnp.arange(adapter_members, dtype=jnp.int32)[None, :]
    select_low = selector.astype(jnp.bfloat16)
    adapter_selector_full = selector.astype(jnp.float32)
    down_rank_rows = lax.all_gather(
        adapter_down_weight.astype(jnp.bfloat16), "wide", axis=1, tiled=True
    )
    up_weight_portion = lax.all_gather(
        adapter_up_weight.astype(jnp.bfloat16), "narrow", axis=1, tiled=True
    )
    up_rank_rows = lax.all_gather(up_weight_portion, "wide", axis=0, tiled=True)
    spread = jnp.dot(tokens, down_rank_rows, preferred_element_type=jnp.float32)
    lowrank_codes = lax.psum(packed_adapter_index(spread, adapter_selector_full), "narrow")
    code_low = lowrank_codes.astype(jnp.bfloat16)
    wide_adapter_index = expand_codes(code_low, select_low)
    summed = lax.psum(
        jnp.dot(tokens, frozen_value_weight, preferred_element_type=jnp.float32), "narrow"
    )
    frozen_value_rows = lax.dynamic_slice_in_dim(summed, row_start, row_count, 0)
    wide_rows = lax.dynamic_slice_in_dim(wide_adapter_index, row_start, row_count, 0)
    rank_output_delta = jnp.dot(wide_rows, up_rank_rows, preferred_element_type=jnp.float32)
    values = (frozen_value_rows + adapter_scale * rank_output_delta).astype(jnp.bfloat16)
    grad_full = lax.all_gather(value_output_gradient, "narrow", axis=0, tiled=True)
    returned_spread_rows = jnp.einsum(
        "tc,kc->tk", grad_full, up_rank_rows, preferred_element_type=jnp.float32
    )
    returned_rank_rows = (
        adapter_scale * packed_adapter_index(returned_spread_rows, adapter_selector_full)
    ).astype(jnp.bfloat16)
    back_wide = expand_codes(returned_rank_rows, select_low)
    grad_tokens = (
        jnp.einsum("tc,dc->td", grad_full, frozen_value_weight, preferred_element_type=jnp.float32)
        + jnp.einsum("tk,dk->td", back_wide, down_rank_rows, preferred_element_type=jnp.float32)
    ).astype(jnp.bfloat16)
    rank_column_count = adapter_up_weight.shape[1]
    grad_columns = lax.dynamic_slice_in_dim(
        grad_full, narrow_index * rank_column_count, rank_column_count, 1
    )
    up_output_term = adapter_scale * jnp.einsum(
        "tk,tc->kc", wide_adapter_index, grad_columns, preferred_element_type=jnp.float32
    )
    up_weight_gradient = lax.psum_scatter(
        up_output_term.astype(jnp.bfloat16), "wide", scatter_dimension=0, tiled=True
    ).astype(jnp.float32)
    down_term = jnp.einsum("td,tk->dk", tokens, back_wide, preferred_element_type=jnp.float32)
    down_weight_gradient = lax.psum_scatter(
        down_term.astype(jnp.bfloat16), "wide", scatter_dimension=1, tiled=True
    ).astype(jnp.float32)
    learning_rate_columns = jnp.repeat(rates, ADAPTER_RANK)
    updated_down_weight, updated_down_moment_first, updated_down_moment_second = apply_adam_moments(
        adapter_down_weight,
        down_moment_first,
        down_moment_second,
        down_weight_gradient,
        learning_rate_columns[None, :],
    )
    updated_up_weight, updated_up_moment_first, updated_up_moment_second = apply_adam_moments(
        adapter_up_weight,
        up_moment_first,
        up_moment_second,
        up_weight_gradient,
        learning_rate_columns[:, None],
    )
    return (
        values,
        grad_tokens,
        updated_down_weight,
        updated_down_moment_first,
        updated_down_moment_second,
        updated_up_weight,
        updated_up_moment_first,
        updated_up_moment_second,
    )


MESH = pl.DeviceIdType.MESH
HALVES = 2


def dot_nn(a, b):
    return lax.dot_general(a, b, (((1,), (0,)), ((), ())), preferred_element_type=jnp.float32)


def dot_nt(a, b):
    return lax.dot_general(a, b, (((1,), (1,)), ((), ())), preferred_element_type=jnp.float32)


def fused_kernel(
    wide,
    tok_hbm, w_hbm, idx_hbm, down_hbm, up_hbm, dm1_hbm, dm2_hbm, um1_hbm, um2_hbm, rates_ref, g_hbm,
    val_out, gt_out, dw_out, dm1_out, dm2_out, uw_out, um1_out, um2_out,
    tok, w, idx, g, upf, downf, dw, dm1, dm2, uw, um1, um2,
    psend, precv, pacc, xsend, xrecv, bsend, brecv, bnat, csend, crecv, cnat,
    dpart, rs_stage, rs_left, rs_right, gt_acc, gt, gu_stage, gu_recv, vals,
    load_sem, store_sem, send_sem, recv_sem,
):
    z = lax.axis_index("wide")
    me = lax.axis_index("narrow")
    x, c = me // 2, me % 2
    xo, co = 1 - x, 1 - c
    block = {0: me, 1: x * 2 + co, 2: xo * 2 + c, 3: xo * 2 + co}
    place = {3: 0, 1: 1, 2: 2, 0: 3}
    order = (3, 1, 2, 0)
    T, D = tok.shape
    C = w.shape[1]
    R, CC = T // 4, C // 4
    K = dw.shape[0]
    A = K * wide
    members = A // ADAPTER_RANK
    HD = D // HALVES

    names = {}

    def number(name):
        return names.setdefault(name, len(names))

    def remote(name, src_ref, dst_ref, device):
        k = number(name)
        return pltpu.make_async_remote_copy(
            src_ref=src_ref, dst_ref=dst_ref, send_sem=send_sem.at[k], recv_sem=recv_sem.at[k],
            device_id=device, device_id_type=MESH,
        )

    sent = []

    def send(name, src_ref, dst_ref, device):
        copy = remote(name, src_ref, dst_ref, device)
        copy.start()
        sent.append(copy)

    def arrived(name, ref):
        remote(name, ref, ref, {"narrow": block[1]}).wait_recv()

    loads = {}

    def load(name, src_ref, dst_ref):
        copy = pltpu.make_async_copy(src_ref, dst_ref, load_sem.at[len(loads)])
        loads[name] = copy
        copy.start()

    stores = []

    def store(src_ref, dst_ref):
        copy = pltpu.make_async_copy(src_ref, dst_ref, store_sem.at[len(stores)])
        stores.append(copy)
        copy.start()

    def rows(m):
        return pl.ds(place[m] * R, R)

    def natural(j):
        return pl.ds(pl.multiple_of(j * R, R), R)

    def column(j):
        return pl.ds(pl.multiple_of(j * CC, CC), CC)

    def shard(j):
        return pl.ds(pl.multiple_of(j * K, K), K)

    def half(h):
        return pl.ds(h * HD, HD)

    load("up", up_hbm, uw)
    load("down", down_hbm, dw)
    load("g", g_hbm, g.at[rows(0)])
    for m in (3, 1):
        load(("tok", m), tok_hbm.at[natural(block[m])], tok.at[rows(m)])
    for q in range(4):
        load(("w", q), w_hbm.at[:, pl.ds(q * CC, CC)], w.at[:, pl.ds(q * CC, CC)])
    for m in (2, 0):
        load(("tok", m), tok_hbm.at[natural(block[m])], tok.at[rows(m)])
    for m in order:
        load(("idx", m), idx_hbm.at[:, natural(block[m])], idx.at[:, rows(m)])
    for name, src_ref, dst_ref in (
        ("dm1", dm1_hbm, dm1), ("dm2", dm2_hbm, dm2), ("um1", um1_hbm, um1), ("um2", um2_hbm, um2)
    ):
        load(name, src_ref, dst_ref)

    barrier = pltpu.get_barrier_semaphore()
    for m in (1, 2, 3):
        pl.semaphore_signal(barrier, inc=1, device_id={"narrow": block[m]}, device_id_type=MESH)
    for d in range(1, wide):
        pl.semaphore_signal(
            barrier, inc=1, device_id={"wide": lax.rem(z + d, wide)}, device_id_type=MESH
        )
    loads["up"].wait()
    upf[shard(z), column(me)] = uw[...].astype(jnp.bfloat16)
    loads["down"].wait()
    downf[shard(z), :] = dw[...].astype(jnp.bfloat16)
    loads["g"].wait()
    pl.semaphore_wait(barrier, 3 + wide - 1)

    for d in range(1, wide):
        mine = upf.at[shard(z), column(me)]
        send(("up", d), mine, mine, {"wide": lax.rem(z + d, wide)})

    chain_sent = []

    def guarded_send(cond, name, src_ref, dst_ref, device):
        copy = remote(name, src_ref, dst_ref, device)
        pl.when(cond)(copy.start)
        chain_sent.append((cond, copy))

    def down_step(s):
        for h in range(HALVES):
            if s >= 1:
                @pl.when(z - s >= 0)
                def _():
                    arrived(("down_r", s - 1, h), downf.at[shard(z - s), half(h)])

            if s <= wide - 2:
                part = downf.at[shard(jnp.maximum(z - s, 0)), half(h)]
                guarded_send(
                    (z - s >= 0) & (z < wide - 1), ("down_r", s, h), part, part,
                    {"wide": jnp.minimum(z + 1, wide - 1)},
                )
            if s >= 1:
                @pl.when(z + s <= wide - 1)
                def _():
                    arrived(("down_l", s - 1, h), downf.at[shard(z + s), half(h)])

            if s <= wide - 2:
                part = downf.at[shard(jnp.minimum(z + s, wide - 1)), half(h)]
                guarded_send(
                    (z + s <= wide - 1) & (z > 0), ("down_l", s, h), part, part,
                    {"wide": jnp.maximum(z - 1, 0)},
                )

    down_step(0)

    for m, core in ((2, c), (3, co)):
        part = column(xo * 2 + core)
        send(("g", m, 0), g.at[rows(0), part], g.at[rows(m), part], {"narrow": block[m]})
    send("g_sib", g.at[rows(0)], g.at[rows(1)], {"narrow": block[1]})
    for m, core in ((2, c), (3, co)):
        part = column(x * 2 + core)
        send(("g", m, 1), g.at[rows(0), part], g.at[rows(m), part], {"narrow": block[m]})

    loads["tok", 3].wait()
    loads["tok", 1].wait()
    for q in range(4):
        loads["w", q].wait()
        cols = pl.ds(q * CC, CC)
        psend[:, cols] = dot_nn(tok[0 : 2 * R, :], w[:, cols]).astype(jnp.bfloat16)
    send("p", psend, precv, {"narrow": block[1]})

    for m in order:
        loads["idx", m].wait()
    adapter = lax.broadcasted_iota(jnp.int32, (A, T), 0) // ADAPTER_RANK

    def member():
        return adapter == jnp.broadcast_to(idx[...], (A, T))

    def pack(full):
        chosen = jnp.where(member(), full, 0.0)
        total = chosen[0:ADAPTER_RANK]
        for a in range(1, members):
            total = total + chosen[a * ADAPTER_RANK : (a + 1) * ADAPTER_RANK]
        return total

    def spread_out(packed):
        return jnp.where(member(), jnp.concatenate([packed] * members, axis=0), 0.0)

    def exchange(name, packed, out, box):
        low = packed.astype(jnp.bfloat16)
        for m in order:
            out[:, natural(block[m])] = low[:, place[m] * R : (place[m] + 1) * R]
        for m in (2, 3, 1):
            send((name, m), out, box.at[m - 1], {"narrow": block[m]})

    def total_of(name, packed, box, nat):
        for m in (1, 2, 3):
            arrived((name, m), box.at[m - 1])
        nat[...] = box[0].astype(jnp.float32) + box[1].astype(jnp.float32) + box[2].astype(jnp.float32)
        return packed + jnp.concatenate([nat[:, natural(block[m])] for m in order], axis=1)

    for d in range(1, wide):
        arrived(("up", d), upf.at[shard(lax.rem(z - d + wide, wide)), column(me)])
    arrived("g_sib", g.at[rows(1)])
    for m in (2, 3):
        arrived(("g", m, 0), g.at[rows(m), column(me)])
    back_part = pack(dot_nt(upf[:, column(me)], g[:, column(me)]))
    exchange("back", back_part, bsend, brecv)
    for m, to in ((2, 3), (3, 2)):
        send(("g_fwd", m, 0), g.at[rows(m), column(me)], g.at[rows(to), column(me)], {"narrow": block[1]})
    for m in (2, 1):
        mine = upf.at[:, column(me)]
        send(("up_x", m), mine, mine, {"narrow": block[m]})

    down_step(1)

    loads["tok", 2].wait()
    loads["tok", 0].wait()
    for q in range(4):
        cols = pl.ds(q * CC, CC)
        pacc[:, cols] = dot_nn(tok[2 * R :, :], w[:, cols])
    arrived("p", precv)
    xsend[...] = (pacc[0:R] + precv[0:R].astype(jnp.float32)).astype(jnp.bfloat16)
    send("px", xsend, xrecv, {"narrow": block[2]})

    back = 2.0 * total_of("back", back_part, brecv, bnat)
    back_wide_t = spread_out(back)
    back_low = back_wide_t.astype(jnp.bfloat16)
    for h in range(HALVES):
        dpart[:, half(h)] = dot_nn(back_low, tok[:, half(h)])

    rs_sent = []

    def rs_step(k):
        for right in (True, False):
            j = wide - 1 - k if right else k
            box = rs_left if right else rs_right
            name = "rs_r" if right else "rs_l"
            ahead = (j > z) if right else (j < z)
            follows = (z > 0) if right else (z < wide - 1)
            target = jnp.minimum(z + 1, wide - 1) if right else jnp.maximum(z - 1, 0)
            for h in range(HALVES):
                own = dpart.at[pl.ds(j * K, K), half(h)]
                stage = rs_stage.at[j, :, half(h)]
                landing = box.at[j, :, half(h)]

                @pl.when(ahead & follows)
                def _():
                    arrived((name, k, h), landing)
                    stage[...] = (own[...] + landing[...].astype(jnp.float32)).astype(jnp.bfloat16)

                @pl.when(ahead & jnp.logical_not(follows))
                def _():
                    stage[...] = own[...].astype(jnp.bfloat16)

                copy = remote((name, k, h), stage, landing, {"wide": target})
                pl.when(ahead)(copy.start)
                rs_sent.append((ahead, copy))

    rs_step(0)
    for s in range(2, wide):
        down_step(s)

    for m, to in ((2, 3), (3, 2)):
        part = column(xo * 2 + c)
        arrived(("g", m, 1), g.at[rows(m), part])
        send(("g_fwd", m, 1), g.at[rows(m), part], g.at[rows(to), part], {"narrow": block[1]})
    arrived(("up_x", 2), upf.at[:, column(block[2])])
    part = upf.at[:, column(block[2])]
    send("up_fwd", part, part, {"narrow": block[1]})

    code_part = pack(dot_nt(tok[...], downf[...]).T)
    exchange("code", code_part, csend, crecv)

    for m in (2, 3):
        arrived(("g_fwd", 5 - m, 0), g.at[rows(m), column(block[1])])
        arrived(("g_fwd", 5 - m, 1), g.at[rows(m), column(block[3])])
    back_rows = back_wide_t.T.astype(jnp.bfloat16)

    def grad_tokens(part, parts):
        width = D // parts
        span = pl.ds(part * width, width)
        gt[:, span] = (dot_nt(g[...], w[span, :]) + dot_nn(back_rows, downf[:, span])).astype(jnp.bfloat16)
        for m in order:
            store(gt.at[rows(m), span], gt_out.at[natural(block[m]), span])

    grad_tokens(0, 4)
    if wide > 2:
        rs_step(1)

    code = total_of("code", code_part, crecv, cnat)
    code_wide_t = spread_out(code)
    code_low = code_wide_t.astype(jnp.bfloat16)
    gu_stage[...] = (2.0 * dot_nn(code_low, g[:, column(me)])).astype(jnp.bfloat16)
    for d in range(1, wide):
        to = lax.rem(z + d, wide)
        send(("gu", d), gu_stage.at[shard(to)], gu_recv.at[d], {"wide": to})

    grad_tokens(1, 4)
    for k in range(2, wide - 1):
        rs_step(k)
    grad_tokens(2, 4)
    grad_tokens(3, 4)

    arrived(("up_x", 1), upf.at[:, column(block[1])])
    arrived("up_fwd", upf.at[:, column(block[3])])
    code_rows = code_wide_t[:, place[0] * R : (place[0] + 1) * R].T.astype(jnp.bfloat16)
    delta = dot_nn(code_rows, upf[...])
    arrived("px", xrecv)
    vals[...] = (
        pacc[R : 2 * R] + precv[R : 2 * R].astype(jnp.float32) + xrecv[...].astype(jnp.float32) + 2.0 * delta
    ).astype(jnp.bfloat16)
    store(vals, val_out)

    owner = lax.broadcasted_iota(jnp.int32, (K, 1), 0) // ADAPTER_RANK
    rate = jnp.zeros((K, 1), jnp.float32)
    for a in range(K // ADAPTER_RANK):
        rate = jnp.where(owner == a, rates_ref[a], rate)

    grad_up = gu_stage[shard(z), :].astype(jnp.float32)
    for d in range(1, wide):
        arrived(("gu", d), gu_recv.at[d])
        grad_up = grad_up + gu_recv[d].astype(jnp.float32)
    loads["um1"].wait()
    loads["um2"].wait()
    uw[...], um1[...], um2[...] = apply_adam_moments(uw[...], um1[...], um2[...], grad_up, rate)
    store(uw, uw_out)
    store(um1, um1_out)
    store(um2, um2_out)

    loads["dm1"].wait()
    loads["dm2"].wait()
    for h in range(HALVES):
        cols = half(h)
        for j in range(wide):
            if j > 0:
                @pl.when(z == j)
                def _():
                    landing = rs_left.at[j, :, cols]
                    arrived(("rs_r", wide - 1 - j, h), landing)
                    own = dpart.at[pl.ds(j * K, K), cols]
                    own[...] = own[...] + landing[...].astype(jnp.float32)

            if j < wide - 1:
                @pl.when(z == j)
                def _():
                    landing = rs_right.at[j, :, cols]
                    arrived(("rs_l", j, h), landing)
                    own = dpart.at[pl.ds(j * K, K), cols]
                    own[...] = own[...] + landing[...].astype(jnp.float32)

        grad_down = dpart[shard(z), cols]
        dw[:, cols], dm1[:, cols], dm2[:, cols] = apply_adam_moments(
            dw[:, cols], dm1[:, cols], dm2[:, cols], grad_down, rate
        )
        store(dw.at[:, cols], dw_out.at[:, cols])
        store(dm1.at[:, cols], dm1_out.at[:, cols])
        store(dm2.at[:, cols], dm2_out.at[:, cols])

    for copy in sent:
        copy.wait_send()
    for cond, copy in chain_sent + rs_sent:
        pl.when(cond)(copy.wait_send)
    for copy in stores:
        copy.wait()


def fused_shards(
    tokens,
    frozen_value_weight,
    token_adapter_index,
    adapter_down_weight,
    adapter_up_weight,
    down_moment_first,
    down_moment_second,
    up_moment_first,
    up_moment_second,
    rates,
    value_output_gradient,
):
    wide = lax.axis_size("wide")
    T, D = tokens.shape
    C = frozen_value_weight.shape[1]
    R, CC = T // 4, C // 4
    K = adapter_down_weight.shape[1]
    A = K * wide
    f32, low = jnp.float32, jnp.bfloat16
    shape = jax.ShapeDtypeStruct
    remotes = 2 * (wide - 1) + 16 + 4 * HALVES * (wide - 1) + 8
    any_spec = pl.BlockSpec(memory_space=pl.ANY)
    outs = pl.pallas_call(
        functools.partial(fused_kernel, wide),
        out_shape=(
            shape((R, C), low), shape((T, D), low),
            shape((K, D), f32), shape((K, D), f32), shape((K, D), f32),
            shape((K, CC), f32), shape((K, CC), f32), shape((K, CC), f32),
        ),
        in_specs=[any_spec] * 9 + [pl.BlockSpec(memory_space=pltpu.SMEM), any_spec],
        out_specs=(any_spec,) * 8,
        scratch_shapes=[
            pltpu.VMEM((T, D), low), pltpu.VMEM((D, C), low), pltpu.VMEM((1, T), jnp.int32),
            pltpu.VMEM((T, C), low), pltpu.VMEM((A, C), low), pltpu.VMEM((A, D), low),
            pltpu.VMEM((K, D), f32), pltpu.VMEM((K, D), f32), pltpu.VMEM((K, D), f32),
            pltpu.VMEM((K, CC), f32), pltpu.VMEM((K, CC), f32), pltpu.VMEM((K, CC), f32),
            pltpu.VMEM((2 * R, C), low), pltpu.VMEM((2 * R, C), low), pltpu.VMEM((2 * R, C), f32),
            pltpu.VMEM((R, C), low), pltpu.VMEM((R, C), low),
            pltpu.VMEM((ADAPTER_RANK, T), low), pltpu.VMEM((3, ADAPTER_RANK, T), low),
            pltpu.VMEM((ADAPTER_RANK, T), f32),
            pltpu.VMEM((ADAPTER_RANK, T), low), pltpu.VMEM((3, ADAPTER_RANK, T), low),
            pltpu.VMEM((ADAPTER_RANK, T), f32),
            pltpu.VMEM((A, D), f32), pltpu.VMEM((wide, K, D), low),
            pltpu.VMEM((wide, K, D), low), pltpu.VMEM((wide, K, D), low),
            pltpu.VMEM((8, 128), f32), pltpu.VMEM((T, D), low),
            pltpu.VMEM((A, CC), low), pltpu.VMEM((wide, K, CC), low), pltpu.VMEM((R, C), low),
            pltpu.SemaphoreType.DMA((20,)), pltpu.SemaphoreType.DMA((16 + 4 + 3 * HALVES,)),
            pltpu.SemaphoreType.DMA((remotes,)), pltpu.SemaphoreType.DMA((remotes,)),
        ],
        compiler_params=pltpu.CompilerParams(
            collective_id=0, has_side_effects=True, vmem_limit_bytes=50 * 1024 * 1024
        ),
        cost_estimate=pl.CostEstimate(
            flops=2 * (2 * T * D * C + 3 * T * D * A), bytes_accessed=12 * 1024 * 1024, transcendentals=0
        ),
    )(
        tokens, frozen_value_weight, token_adapter_index.reshape(1, T),
        adapter_down_weight.T, adapter_up_weight,
        down_moment_first.T, down_moment_second.T, up_moment_first, up_moment_second,
        rates, value_output_gradient,
    )
    values, grad_tokens, dw, dm1, dm2, uw, um1, um2 = outs
    return (values, grad_tokens, dw.T, dm1.T, dm2.T, uw, um1, um2)


def solution(mesh):
    return jax.shard_map(
        fused_shards if mesh.shape["narrow"] == 4 and mesh.shape["wide"] > 1 else shards,
        mesh=mesh,
        in_specs=(
            P(("grid", "wide"), "narrow"),
            P("narrow", None),
            P(("grid", "wide"), None),
            P(("grid", "narrow"), "wide"),
            P(("grid", "wide"), "narrow"),
            P(("grid", "narrow"), "wide"),
            P(("grid", "narrow"), "wide"),
            P(("grid", "wide"), "narrow"),
            P(("grid", "wide"), "narrow"),
            P(("grid", "wide")),
            P(("grid", "wide", "narrow"), None),
        ),
        out_specs=(
            P(("grid", "wide", "narrow"), None),
            P(("grid", "wide"), "narrow"),
            P(("grid", "narrow"), "wide"),
            P(("grid", "narrow"), "wide"),
            P(("grid", "narrow"), "wide"),
            P(("grid", "wide"), "narrow"),
            P(("grid", "wide"), "narrow"),
            P(("grid", "wide"), "narrow"),
        ),
        check_vma=False,
    )
```

```python
import functools

import jax
import jax.numpy as jnp
from jax import lax
from jax.experimental import pallas as pl
from jax.experimental.pallas import tpu as pltpu
from jax.sharding import PartitionSpec as P

ADAPTER_RANK = 16
STEP = 1000


adapter_scale = 2.0
beta_first = 0.9
beta_second = 0.999
adam_eps = 1e-08


def expand_codes(lowrank, selector):
    item_count = lowrank.shape[0]
    return (selector[:, :, None] * lowrank[:, None, :]).reshape(item_count, -1)


def packed_adapter_index(spread, selector):
    item_count = spread.shape[0]
    return jnp.sum(spread.reshape(item_count, selector.shape[1], -1) * selector[:, :, None], axis=1)


def apply_adam_moments(parameter, first, second, gradient, step_rate):
    first_new = beta_first * first + (1.0 - beta_first) * gradient
    second_new = beta_second * second + (1.0 - beta_second) * gradient * gradient
    first_fix = 1.0 - beta_first**STEP
    second_fix = 1.0 - beta_second**STEP
    update = step_rate * (first_new / first_fix) / (jnp.sqrt(second_new / second_fix) + adam_eps)
    return (parameter - update, first_new, second_new)


def shards(
    tokens,
    frozen_value_weight,
    token_adapter_index,
    adapter_down_weight,
    adapter_up_weight,
    down_moment_first,
    down_moment_second,
    up_moment_first,
    up_moment_second,
    rates,
    value_output_gradient,
):
    wide_adapter_count = lax.axis_size("wide")
    narrow_count = lax.axis_size("narrow")
    narrow_index = lax.axis_index("narrow")
    token_count = tokens.shape[0]
    row_count = token_count // narrow_count
    row_start = narrow_index * row_count
    adapter_members = adapter_down_weight.shape[1] * wide_adapter_count // ADAPTER_RANK
    selector = token_adapter_index == jnp.arange(adapter_members, dtype=jnp.int32)[None, :]
    select_low = selector.astype(jnp.bfloat16)
    adapter_selector_full = selector.astype(jnp.float32)
    down_rank_rows = lax.all_gather(
        adapter_down_weight.astype(jnp.bfloat16), "wide", axis=1, tiled=True
    )
    up_weight_portion = lax.all_gather(
        adapter_up_weight.astype(jnp.bfloat16), "narrow", axis=1, tiled=True
    )
    up_rank_rows = lax.all_gather(up_weight_portion, "wide", axis=0, tiled=True)
    spread = jnp.dot(tokens, down_rank_rows, preferred_element_type=jnp.float32)
    lowrank_codes = lax.psum(packed_adapter_index(spread, adapter_selector_full), "narrow")
    code_low = lowrank_codes.astype(jnp.bfloat16)
    wide_adapter_index = expand_codes(code_low, select_low)
    summed = lax.psum(
        jnp.dot(tokens, frozen_value_weight, preferred_element_type=jnp.float32), "narrow"
    )
    frozen_value_rows = lax.dynamic_slice_in_dim(summed, row_start, row_count, 0)
    wide_rows = lax.dynamic_slice_in_dim(wide_adapter_index, row_start, row_count, 0)
    rank_output_delta = jnp.dot(wide_rows, up_rank_rows, preferred_element_type=jnp.float32)
    values = (frozen_value_rows + adapter_scale * rank_output_delta).astype(jnp.bfloat16)
    grad_full = lax.all_gather(value_output_gradient, "narrow", axis=0, tiled=True)
    returned_spread_rows = jnp.einsum(
        "tc,kc->tk", grad_full, up_rank_rows, preferred_element_type=jnp.float32
    )
    returned_rank_rows = (
        adapter_scale * packed_adapter_index(returned_spread_rows, adapter_selector_full)
    ).astype(jnp.bfloat16)
    back_wide = expand_codes(returned_rank_rows, select_low)
    grad_tokens = (
        jnp.einsum("tc,dc->td", grad_full, frozen_value_weight, preferred_element_type=jnp.float32)
        + jnp.einsum("tk,dk->td", back_wide, down_rank_rows, preferred_element_type=jnp.float32)
    ).astype(jnp.bfloat16)
    rank_column_count = adapter_up_weight.shape[1]
    grad_columns = lax.dynamic_slice_in_dim(
        grad_full, narrow_index * rank_column_count, rank_column_count, 1
    )
    up_output_term = adapter_scale * jnp.einsum(
        "tk,tc->kc", wide_adapter_index, grad_columns, preferred_element_type=jnp.float32
    )
    up_weight_gradient = lax.psum_scatter(
        up_output_term.astype(jnp.bfloat16), "wide", scatter_dimension=0, tiled=True
    ).astype(jnp.float32)
    down_term = jnp.einsum("td,tk->dk", tokens, back_wide, preferred_element_type=jnp.float32)
    down_weight_gradient = lax.psum_scatter(
        down_term.astype(jnp.bfloat16), "wide", scatter_dimension=1, tiled=True
    ).astype(jnp.float32)
    learning_rate_columns = jnp.repeat(rates, ADAPTER_RANK)
    updated_down_weight, updated_down_moment_first, updated_down_moment_second = apply_adam_moments(
        adapter_down_weight,
        down_moment_first,
        down_moment_second,
        down_weight_gradient,
        learning_rate_columns[None, :],
    )
    updated_up_weight, updated_up_moment_first, updated_up_moment_second = apply_adam_moments(
        adapter_up_weight,
        up_moment_first,
        up_moment_second,
        up_weight_gradient,
        learning_rate_columns[:, None],
    )
    return (
        values,
        grad_tokens,
        updated_down_weight,
        updated_down_moment_first,
        updated_down_moment_second,
        updated_up_weight,
        updated_up_moment_first,
        updated_up_moment_second,
    )


MESH = pl.DeviceIdType.MESH
HALVES = 2


def dot_nn(a, b):
    return lax.dot_general(a, b, (((1,), (0,)), ((), ())), preferred_element_type=jnp.float32)


def dot_nt(a, b):
    return lax.dot_general(a, b, (((1,), (1,)), ((), ())), preferred_element_type=jnp.float32)


def fused_kernel(
    wide,
    tok_hbm, w_hbm, idx_hbm, down_hbm, up_hbm, dm1_hbm, dm2_hbm, um1_hbm, um2_hbm, rates_hbm, g_hbm,
    val_out, gt_out, dw_out, dm1_out, dm2_out, uw_out, um1_out, um2_out,
    tok, w, idx, g, upf, downf, dw, dm1, dm2, uw, um1, um2,
    psend, precv, pacc, xsend, xrecv, bsend, brecv, bnat, csend, crecv, cnat,
    dpart, rs_stage, rs_left, rs_right, gt_acc, gt, gu_stage, gu_recv, vals, rates_ref,
    load_sem, store_sem, send_sem, recv_sem,
):
    z = lax.axis_index("wide")
    me = lax.axis_index("narrow")
    x, c = me // 2, me % 2
    xo, co = 1 - x, 1 - c
    block = {0: me, 1: x * 2 + co, 2: xo * 2 + c, 3: xo * 2 + co}
    place = {3: 0, 1: 1, 2: 2, 0: 3}
    order = (3, 1, 2, 0)
    T, D = tok.shape
    C = w.shape[1]
    R, CC = T // 4, C // 4
    K = dw.shape[0]
    A = K * wide
    members = A // ADAPTER_RANK
    HD = D // HALVES

    names = {}

    def number(name):
        return names.setdefault(name, len(names))

    def remote(name, src_ref, dst_ref, device):
        k = number(name)
        return pltpu.make_async_remote_copy(
            src_ref=src_ref, dst_ref=dst_ref, send_sem=send_sem.at[k], recv_sem=recv_sem.at[k],
            device_id=device, device_id_type=MESH,
        )

    sent = []

    def send(name, src_ref, dst_ref, device):
        copy = remote(name, src_ref, dst_ref, device)
        copy.start()
        sent.append(copy)

    def arrived(name, ref):
        remote(name, ref, ref, {"narrow": block[1]}).wait_recv()

    loads = {}

    def load(name, src_ref, dst_ref):
        copy = pltpu.make_async_copy(src_ref, dst_ref, load_sem.at[len(loads)])
        loads[name] = copy
        copy.start()

    stores = []

    def store(src_ref, dst_ref):
        copy = pltpu.make_async_copy(src_ref, dst_ref, store_sem.at[len(stores)])
        stores.append(copy)
        copy.start()

    def rows(m):
        return pl.ds(place[m] * R, R)

    def natural(j):
        return pl.ds(pl.multiple_of(j * R, R), R)

    def column(j):
        return pl.ds(pl.multiple_of(j * CC, CC), CC)

    def shard(j):
        return pl.ds(pl.multiple_of(j * K, K), K)

    def half(h):
        return pl.ds(h * HD, HD)

    load("up", up_hbm, uw)
    load("down", down_hbm, dw)
    load("g", g_hbm, g.at[rows(0)])
    for m in (3, 1):
        load(("tok", m), tok_hbm.at[natural(block[m])], tok.at[rows(m)])
    for q in range(4):
        load(("w", q), w_hbm.at[:, pl.ds(q * CC, CC)], w.at[:, pl.ds(q * CC, CC)])
    for m in (2, 0):
        load(("tok", m), tok_hbm.at[natural(block[m])], tok.at[rows(m)])
    for m in order:
        load(("idx", m), idx_hbm.at[:, natural(block[m])], idx.at[:, rows(m)])
    for name, src_ref, dst_ref in (
        ("dm1", dm1_hbm, dm1), ("dm2", dm2_hbm, dm2), ("um1", um1_hbm, um1), ("um2", um2_hbm, um2),
        ("rates", rates_hbm, rates_ref),
    ):
        load(name, src_ref, dst_ref)

    barrier = pltpu.get_barrier_semaphore()
    for m in (1, 2, 3):
        pl.semaphore_signal(barrier, inc=1, device_id={"narrow": block[m]}, device_id_type=MESH)
    for d in range(1, wide):
        pl.semaphore_signal(
            barrier, inc=1, device_id={"wide": lax.rem(z + d, wide)}, device_id_type=MESH
        )
    loads["up"].wait()
    upf[shard(z), column(me)] = uw[...].astype(jnp.bfloat16)
    loads["down"].wait()
    downf[shard(z), :] = dw[...].astype(jnp.bfloat16)
    loads["g"].wait()
    pl.semaphore_wait(barrier, 3 + wide - 1)

    for d in range(1, wide):
        mine = upf.at[shard(z), column(me)]
        send(("up", d), mine, mine, {"wide": lax.rem(z + d, wide)})

    chain_sent = []

    def guarded_send(cond, name, src_ref, dst_ref, device):
        copy = remote(name, src_ref, dst_ref, device)
        pl.when(cond)(copy.start)
        chain_sent.append((cond, copy))

    def down_step(s):
        for h in range(HALVES):
            if s >= 1:
                @pl.when(z - s >= 0)
                def _():
                    arrived(("down_r", s - 1, h), downf.at[shard(z - s), half(h)])

            if s <= wide - 2:
                part = downf.at[shard(jnp.maximum(z - s, 0)), half(h)]
                guarded_send(
                    (z - s >= 0) & (z < wide - 1), ("down_r", s, h), part, part,
                    {"wide": jnp.minimum(z + 1, wide - 1)},
                )
            if s >= 1:
                @pl.when(z + s <= wide - 1)
                def _():
                    arrived(("down_l", s - 1, h), downf.at[shard(z + s), half(h)])

            if s <= wide - 2:
                part = downf.at[shard(jnp.minimum(z + s, wide - 1)), half(h)]
                guarded_send(
                    (z + s <= wide - 1) & (z > 0), ("down_l", s, h), part, part,
                    {"wide": jnp.maximum(z - 1, 0)},
                )

    down_step(0)

    for m, core in ((2, c), (3, co)):
        part = column(xo * 2 + core)
        send(("g", m, 0), g.at[rows(0), part], g.at[rows(m), part], {"narrow": block[m]})
    send("g_sib", g.at[rows(0)], g.at[rows(1)], {"narrow": block[1]})
    for m, core in ((2, c), (3, co)):
        part = column(x * 2 + core)
        send(("g", m, 1), g.at[rows(0), part], g.at[rows(m), part], {"narrow": block[m]})

    loads["tok", 3].wait()
    loads["tok", 1].wait()
    for q in range(4):
        loads["w", q].wait()
        cols = pl.ds(q * CC, CC)
        psend[:, cols] = dot_nn(tok[0 : 2 * R, :], w[:, cols]).astype(jnp.bfloat16)
    send("p", psend, precv, {"narrow": block[1]})

    for m in order:
        loads["idx", m].wait()
    adapter = lax.broadcasted_iota(jnp.int32, (A, T), 0) // ADAPTER_RANK

    def member():
        return adapter == jnp.broadcast_to(idx[...], (A, T))

    def pack(full):
        chosen = jnp.where(member(), full, 0.0)
        total = chosen[0:ADAPTER_RANK]
        for a in range(1, members):
            total = total + chosen[a * ADAPTER_RANK : (a + 1) * ADAPTER_RANK]
        return total

    def spread_out(packed):
        return jnp.where(member(), jnp.concatenate([packed] * members, axis=0), 0.0)

    def exchange(name, packed, out, box):
        low = packed.astype(jnp.bfloat16)
        for m in order:
            out[:, natural(block[m])] = low[:, place[m] * R : (place[m] + 1) * R]
        for m in (2, 3, 1):
            send((name, m), out, box.at[m - 1], {"narrow": block[m]})

    def total_of(name, packed, box, nat):
        for m in (1, 2, 3):
            arrived((name, m), box.at[m - 1])
        nat[...] = box[0].astype(jnp.float32) + box[1].astype(jnp.float32) + box[2].astype(jnp.float32)
        return packed + jnp.concatenate([nat[:, natural(block[m])] for m in order], axis=1)

    for d in range(1, wide):
        arrived(("up", d), upf.at[shard(lax.rem(z - d + wide, wide)), column(me)])
    arrived("g_sib", g.at[rows(1)])
    for m in (2, 3):
        arrived(("g", m, 0), g.at[rows(m), column(me)])
    back_part = pack(dot_nt(upf[:, column(me)], g[:, column(me)]))
    exchange("back", back_part, bsend, brecv)
    for m, to in ((2, 3), (3, 2)):
        send(("g_fwd", m, 0), g.at[rows(m), column(me)], g.at[rows(to), column(me)], {"narrow": block[1]})
    for m in (2, 1):
        mine = upf.at[:, column(me)]
        send(("up_x", m), mine, mine, {"narrow": block[m]})

    down_step(1)

    loads["tok", 2].wait()
    loads["tok", 0].wait()
    for q in range(4):
        cols = pl.ds(q * CC, CC)
        pacc[:, cols] = dot_nn(tok[2 * R :, :], w[:, cols])
    arrived("p", precv)
    xsend[...] = (pacc[0:R] + precv[0:R].astype(jnp.float32)).astype(jnp.bfloat16)
    send("px", xsend, xrecv, {"narrow": block[2]})

    back = 2.0 * total_of("back", back_part, brecv, bnat)
    back_wide_t = spread_out(back)
    back_low = back_wide_t.astype(jnp.bfloat16)
    for h in range(HALVES):
        dpart[:, half(h)] = dot_nn(back_low, tok[:, half(h)])

    rs_sent = []

    def rs_step(k):
        for right in (True, False):
            j = wide - 1 - k if right else k
            box = rs_left if right else rs_right
            name = "rs_r" if right else "rs_l"
            ahead = (j > z) if right else (j < z)
            follows = (z > 0) if right else (z < wide - 1)
            target = jnp.minimum(z + 1, wide - 1) if right else jnp.maximum(z - 1, 0)
            for h in range(HALVES):
                own = dpart.at[pl.ds(j * K, K), half(h)]
                stage = rs_stage.at[j, :, half(h)]
                landing = box.at[j, :, half(h)]

                @pl.when(ahead & follows)
                def _():
                    arrived((name, k, h), landing)
                    stage[...] = (own[...] + landing[...].astype(jnp.float32)).astype(jnp.bfloat16)

                @pl.when(ahead & jnp.logical_not(follows))
                def _():
                    stage[...] = own[...].astype(jnp.bfloat16)

                copy = remote((name, k, h), stage, landing, {"wide": target})
                pl.when(ahead)(copy.start)
                rs_sent.append((ahead, copy))

    rs_step(0)
    for s in range(2, wide):
        down_step(s)

    for m, to in ((2, 3), (3, 2)):
        part = column(xo * 2 + c)
        arrived(("g", m, 1), g.at[rows(m), part])
        send(("g_fwd", m, 1), g.at[rows(m), part], g.at[rows(to), part], {"narrow": block[1]})
    arrived(("up_x", 2), upf.at[:, column(block[2])])
    part = upf.at[:, column(block[2])]
    send("up_fwd", part, part, {"narrow": block[1]})

    code_part = pack(dot_nt(tok[...], downf[...]).T)
    exchange("code", code_part, csend, crecv)

    for m in (2, 3):
        arrived(("g_fwd", 5 - m, 0), g.at[rows(m), column(block[1])])
        arrived(("g_fwd", 5 - m, 1), g.at[rows(m), column(block[3])])
    back_rows = back_wide_t.T.astype(jnp.bfloat16)

    def grad_tokens(part, parts):
        width = D // parts
        span = pl.ds(part * width, width)
        gt[:, span] = (dot_nt(g[...], w[span, :]) + dot_nn(back_rows, downf[:, span])).astype(jnp.bfloat16)
        for m in order:
            store(gt.at[rows(m), span], gt_out.at[natural(block[m]), span])

    grad_tokens(0, 4)
    if wide > 2:
        rs_step(1)

    code = total_of("code", code_part, crecv, cnat)
    code_wide_t = spread_out(code)
    code_low = code_wide_t.astype(jnp.bfloat16)
    gu_stage[...] = (2.0 * dot_nn(code_low, g[:, column(me)])).astype(jnp.bfloat16)
    for d in range(1, wide):
        to = lax.rem(z + d, wide)
        send(("gu", d), gu_stage.at[shard(to)], gu_recv.at[d], {"wide": to})

    grad_tokens(1, 4)
    for k in range(2, wide - 1):
        rs_step(k)
    grad_tokens(2, 4)
    grad_tokens(3, 4)

    arrived(("up_x", 1), upf.at[:, column(block[1])])
    arrived("up_fwd", upf.at[:, column(block[3])])
    code_rows = code_wide_t[:, place[0] * R : (place[0] + 1) * R].T.astype(jnp.bfloat16)
    delta = dot_nn(code_rows, upf[...])
    arrived("px", xrecv)
    vals[...] = (
        pacc[R : 2 * R] + precv[R : 2 * R].astype(jnp.float32) + xrecv[...].astype(jnp.float32) + 2.0 * delta
    ).astype(jnp.bfloat16)
    store(vals, val_out)

    loads["rates"].wait()
    owner = lax.broadcasted_iota(jnp.int32, (K, 1), 0) // ADAPTER_RANK
    rate = jnp.zeros((K, 1), jnp.float32)
    for a in range(K // ADAPTER_RANK):
        rate = jnp.where(owner == a, rates_ref[a], rate)

    grad_up = gu_stage[shard(z), :].astype(jnp.float32)
    for d in range(1, wide):
        arrived(("gu", d), gu_recv.at[d])
        grad_up = grad_up + gu_recv[d].astype(jnp.float32)
    loads["um1"].wait()
    loads["um2"].wait()
    uw[...], um1[...], um2[...] = apply_adam_moments(uw[...], um1[...], um2[...], grad_up, rate)
    store(uw, uw_out)
    store(um1, um1_out)
    store(um2, um2_out)

    loads["dm1"].wait()
    loads["dm2"].wait()
    for h in range(HALVES):
        cols = half(h)
        for j in range(wide):
            if j > 0:
                @pl.when(z == j)
                def _():
                    landing = rs_left.at[j, :, cols]
                    arrived(("rs_r", wide - 1 - j, h), landing)
                    own = dpart.at[pl.ds(j * K, K), cols]
                    own[...] = own[...] + landing[...].astype(jnp.float32)

            if j < wide - 1:
                @pl.when(z == j)
                def _():
                    landing = rs_right.at[j, :, cols]
                    arrived(("rs_l", j, h), landing)
                    own = dpart.at[pl.ds(j * K, K), cols]
                    own[...] = own[...] + landing[...].astype(jnp.float32)

        grad_down = dpart[shard(z), cols]
        dw[:, cols], dm1[:, cols], dm2[:, cols] = apply_adam_moments(
            dw[:, cols], dm1[:, cols], dm2[:, cols], grad_down, rate
        )
        store(dw.at[:, cols], dw_out.at[:, cols])
        store(dm1.at[:, cols], dm1_out.at[:, cols])
        store(dm2.at[:, cols], dm2_out.at[:, cols])

    for copy in sent:
        copy.wait_send()
    for cond, copy in chain_sent + rs_sent:
        pl.when(cond)(copy.wait_send)
    for copy in stores:
        copy.wait()


def write_kernel(*refs):
    held, load_sem, store_sem = refs[16:24], refs[24], refs[25]
    parts = 4
    pieces = []
    for k in (1, 0, 2, 3, 4, 5, 6, 7):
        cuts = parts if k == 1 else 1
        size = refs[k].shape[0] // cuts
        for part in range(cuts):
            rows, n = pl.ds(part * size, size), len(pieces)
            pieces.append((
                pltpu.make_async_copy(refs[k].at[rows], held[k].at[rows], load_sem.at[n]),
                pltpu.make_async_copy(held[k].at[rows], refs[8 + k].at[rows], store_sem.at[n]),
            ))
    for load, _ in pieces:
        load.start()
    for load, store in pieces:
        load.wait()
        store.start()
    for _, store in pieces:
        store.wait()


def fused_shards(
    tokens,
    frozen_value_weight,
    token_adapter_index,
    adapter_down_weight,
    adapter_up_weight,
    down_moment_first,
    down_moment_second,
    up_moment_first,
    up_moment_second,
    rates,
    value_output_gradient,
):
    wide = lax.axis_size("wide")
    T, D = tokens.shape
    C = frozen_value_weight.shape[1]
    R, CC = T // 4, C // 4
    K = adapter_down_weight.shape[1]
    A = K * wide
    f32, low = jnp.float32, jnp.bfloat16
    shape = jax.ShapeDtypeStruct
    remotes = 2 * (wide - 1) + 16 + 4 * HALVES * (wide - 1) + 8
    any_spec = pl.BlockSpec(memory_space=pl.ANY)
    hbm_spec = pl.BlockSpec(memory_space=pltpu.HBM)
    outs = pl.pallas_call(
        functools.partial(fused_kernel, wide),
        out_shape=(
            shape((R, C), low), shape((T, D), low),
            shape((K, D), f32), shape((K, D), f32), shape((K, D), f32),
            shape((K, CC), f32), shape((K, CC), f32), shape((K, CC), f32),
        ),
        in_specs=[hbm_spec] * 11,
        out_specs=(any_spec,) * 8,
        scratch_shapes=[
            pltpu.VMEM((T, D), low), pltpu.VMEM((D, C), low), pltpu.VMEM((1, T), jnp.int32),
            pltpu.VMEM((T, C), low), pltpu.VMEM((A, C), low), pltpu.VMEM((A, D), low),
            pltpu.VMEM((K, D), f32), pltpu.VMEM((K, D), f32), pltpu.VMEM((K, D), f32),
            pltpu.VMEM((K, CC), f32), pltpu.VMEM((K, CC), f32), pltpu.VMEM((K, CC), f32),
            pltpu.VMEM((2 * R, C), low), pltpu.VMEM((2 * R, C), low), pltpu.VMEM((2 * R, C), f32),
            pltpu.VMEM((R, C), low), pltpu.VMEM((R, C), low),
            pltpu.VMEM((ADAPTER_RANK, T), low), pltpu.VMEM((3, ADAPTER_RANK, T), low),
            pltpu.VMEM((ADAPTER_RANK, T), f32),
            pltpu.VMEM((ADAPTER_RANK, T), low), pltpu.VMEM((3, ADAPTER_RANK, T), low),
            pltpu.VMEM((ADAPTER_RANK, T), f32),
            pltpu.VMEM((A, D), f32), pltpu.VMEM((wide, K, D), low),
            pltpu.VMEM((wide, K, D), low), pltpu.VMEM((wide, K, D), low),
            pltpu.VMEM((8, 128), f32), pltpu.VMEM((T, D), low),
            pltpu.VMEM((A, CC), low), pltpu.VMEM((wide, K, CC), low), pltpu.VMEM((R, C), low),
            pltpu.SMEM(rates.shape, f32),
            pltpu.SemaphoreType.DMA((20,)), pltpu.SemaphoreType.DMA((16 + 4 + 3 * HALVES,)),
            pltpu.SemaphoreType.DMA((remotes,)), pltpu.SemaphoreType.DMA((remotes,)),
        ],
        compiler_params=pltpu.CompilerParams(
            collective_id=0, has_side_effects=True, vmem_limit_bytes=64 * 1024 * 1024 - 65536
        ),
        cost_estimate=pl.CostEstimate(
            flops=2 * (2 * T * D * C + 3 * T * D * A), bytes_accessed=12 * 1024 * 1024, transcendentals=0
        ),
    )(
        tokens, frozen_value_weight, token_adapter_index.reshape(1, T),
        adapter_down_weight.T, adapter_up_weight,
        down_moment_first.T, down_moment_second.T, up_moment_first, up_moment_second,
        rates, value_output_gradient,
    )
    values, grad_tokens, dw, dm1, dm2, uw, um1, um2 = pl.pallas_call(
        write_kernel,
        out_shape=tuple(shape(a.shape, a.dtype) for a in outs),
        in_specs=[any_spec] * 8,
        out_specs=(hbm_spec,) * 8,
        scratch_shapes=[pltpu.VMEM(a.shape, a.dtype) for a in outs]
        + [pltpu.SemaphoreType.DMA((11,)), pltpu.SemaphoreType.DMA((11,))],
    )(*outs)
    return (values, grad_tokens, dw.T, dm1.T, dm2.T, uw, um1, um2)


def solution(mesh):
    return jax.shard_map(
        fused_shards if mesh.shape["narrow"] == 4 and mesh.shape["wide"] > 1 else shards,
        mesh=mesh,
        in_specs=(
            P(("grid", "wide"), "narrow"),
            P("narrow", None),
            P(("grid", "wide"), None),
            P(("grid", "narrow"), "wide"),
            P(("grid", "wide"), "narrow"),
            P(("grid", "narrow"), "wide"),
            P(("grid", "narrow"), "wide"),
            P(("grid", "wide"), "narrow"),
            P(("grid", "wide"), "narrow"),
            P(("grid", "wide")),
            P(("grid", "wide", "narrow"), None),
        ),
        out_specs=(
            P(("grid", "wide", "narrow"), None),
            P(("grid", "wide"), "narrow"),
            P(("grid", "narrow"), "wide"),
            P(("grid", "narrow"), "wide"),
            P(("grid", "narrow"), "wide"),
            P(("grid", "wide"), "narrow"),
            P(("grid", "wide"), "narrow"),
            P(("grid", "wide"), "narrow"),
        ),
        check_vma=False,
    )
```

```python
import functools

import jax
import jax.numpy as jnp
from jax import lax
from jax.experimental import pallas as pl
from jax.experimental.pallas import tpu as pltpu
from jax.sharding import PartitionSpec as P

ADAPTER_RANK = 16
STEP = 1000


adapter_scale = 2.0
beta_first = 0.9
beta_second = 0.999
adam_eps = 1e-08


def expand_codes(lowrank, selector):
    item_count = lowrank.shape[0]
    return (selector[:, :, None] * lowrank[:, None, :]).reshape(item_count, -1)


def packed_adapter_index(spread, selector):
    item_count = spread.shape[0]
    return jnp.sum(spread.reshape(item_count, selector.shape[1], -1) * selector[:, :, None], axis=1)


def apply_adam_moments(parameter, first, second, gradient, step_rate):
    first_new = beta_first * first + (1.0 - beta_first) * gradient
    second_new = beta_second * second + (1.0 - beta_second) * gradient * gradient
    first_fix = 1.0 - beta_first**STEP
    second_fix = 1.0 - beta_second**STEP
    update = step_rate * (first_new / first_fix) / (jnp.sqrt(second_new / second_fix) + adam_eps)
    return (parameter - update, first_new, second_new)


def shards(
    tokens,
    frozen_value_weight,
    token_adapter_index,
    adapter_down_weight,
    adapter_up_weight,
    down_moment_first,
    down_moment_second,
    up_moment_first,
    up_moment_second,
    rates,
    value_output_gradient,
):
    wide_adapter_count = lax.axis_size("wide")
    narrow_count = lax.axis_size("narrow")
    narrow_index = lax.axis_index("narrow")
    token_count = tokens.shape[0]
    row_count = token_count // narrow_count
    row_start = narrow_index * row_count
    adapter_members = adapter_down_weight.shape[1] * wide_adapter_count // ADAPTER_RANK
    selector = token_adapter_index == jnp.arange(adapter_members, dtype=jnp.int32)[None, :]
    select_low = selector.astype(jnp.bfloat16)
    adapter_selector_full = selector.astype(jnp.float32)
    down_rank_rows = lax.all_gather(
        adapter_down_weight.astype(jnp.bfloat16), "wide", axis=1, tiled=True
    )
    up_weight_portion = lax.all_gather(
        adapter_up_weight.astype(jnp.bfloat16), "narrow", axis=1, tiled=True
    )
    up_rank_rows = lax.all_gather(up_weight_portion, "wide", axis=0, tiled=True)
    spread = jnp.dot(tokens, down_rank_rows, preferred_element_type=jnp.float32)
    lowrank_codes = lax.psum(packed_adapter_index(spread, adapter_selector_full), "narrow")
    code_low = lowrank_codes.astype(jnp.bfloat16)
    wide_adapter_index = expand_codes(code_low, select_low)
    summed = lax.psum(
        jnp.dot(tokens, frozen_value_weight, preferred_element_type=jnp.float32), "narrow"
    )
    frozen_value_rows = lax.dynamic_slice_in_dim(summed, row_start, row_count, 0)
    wide_rows = lax.dynamic_slice_in_dim(wide_adapter_index, row_start, row_count, 0)
    rank_output_delta = jnp.dot(wide_rows, up_rank_rows, preferred_element_type=jnp.float32)
    values = (frozen_value_rows + adapter_scale * rank_output_delta).astype(jnp.bfloat16)
    grad_full = lax.all_gather(value_output_gradient, "narrow", axis=0, tiled=True)
    returned_spread_rows = jnp.einsum(
        "tc,kc->tk", grad_full, up_rank_rows, preferred_element_type=jnp.float32
    )
    returned_rank_rows = (
        adapter_scale * packed_adapter_index(returned_spread_rows, adapter_selector_full)
    ).astype(jnp.bfloat16)
    back_wide = expand_codes(returned_rank_rows, select_low)
    grad_tokens = (
        jnp.einsum("tc,dc->td", grad_full, frozen_value_weight, preferred_element_type=jnp.float32)
        + jnp.einsum("tk,dk->td", back_wide, down_rank_rows, preferred_element_type=jnp.float32)
    ).astype(jnp.bfloat16)
    rank_column_count = adapter_up_weight.shape[1]
    grad_columns = lax.dynamic_slice_in_dim(
        grad_full, narrow_index * rank_column_count, rank_column_count, 1
    )
    up_output_term = adapter_scale * jnp.einsum(
        "tk,tc->kc", wide_adapter_index, grad_columns, preferred_element_type=jnp.float32
    )
    up_weight_gradient = lax.psum_scatter(
        up_output_term.astype(jnp.bfloat16), "wide", scatter_dimension=0, tiled=True
    ).astype(jnp.float32)
    down_term = jnp.einsum("td,tk->dk", tokens, back_wide, preferred_element_type=jnp.float32)
    down_weight_gradient = lax.psum_scatter(
        down_term.astype(jnp.bfloat16), "wide", scatter_dimension=1, tiled=True
    ).astype(jnp.float32)
    learning_rate_columns = jnp.repeat(rates, ADAPTER_RANK)
    updated_down_weight, updated_down_moment_first, updated_down_moment_second = apply_adam_moments(
        adapter_down_weight,
        down_moment_first,
        down_moment_second,
        down_weight_gradient,
        learning_rate_columns[None, :],
    )
    updated_up_weight, updated_up_moment_first, updated_up_moment_second = apply_adam_moments(
        adapter_up_weight,
        up_moment_first,
        up_moment_second,
        up_weight_gradient,
        learning_rate_columns[:, None],
    )
    return (
        values,
        grad_tokens,
        updated_down_weight,
        updated_down_moment_first,
        updated_down_moment_second,
        updated_up_weight,
        updated_up_moment_first,
        updated_up_moment_second,
    )


MESH = pl.DeviceIdType.MESH
HALVES = 2


def dot_nn(a, b):
    return lax.dot_general(a, b, (((1,), (0,)), ((), ())), preferred_element_type=jnp.float32)


def dot_nt(a, b):
    return lax.dot_general(a, b, (((1,), (1,)), ((), ())), preferred_element_type=jnp.float32)


def fused_kernel(
    wide,
    tok_hbm, w_hbm, idx_hbm, down_hbm, up_hbm, dm1_hbm, dm2_hbm, um1_hbm, um2_hbm, rates_hbm, g_hbm,
    val_out, gt_out, dw_out, dm1_out, dm2_out, uw_out, um1_out, um2_out,
    tok, w, idx, g, upf, downf, dw, dm1, dm2, uw, um1, um2,
    psend, precv, pacc, xsend, xrecv, bsend, brecv, bnat, csend, crecv, cnat,
    dpart, rs_stage, rs_left, rs_right, gt_acc, gt, gu_stage, gu_recv, vals, rates_ref,
    load_sem, store_sem, send_sem, recv_sem,
):
    z = lax.axis_index("wide")
    me = lax.axis_index("narrow")
    x, c = me // 2, me % 2
    xo, co = 1 - x, 1 - c
    block = {0: me, 1: x * 2 + co, 2: xo * 2 + c, 3: xo * 2 + co}
    place = {3: 0, 1: 1, 2: 2, 0: 3}
    order = (3, 1, 2, 0)
    T, D = tok.shape
    C = w.shape[1]
    R, CC = T // 4, C // 4
    K = dw.shape[0]
    A = K * wide
    members = A // ADAPTER_RANK
    HD = D // HALVES

    names = {}

    def number(name):
        return names.setdefault(name, len(names))

    def remote(name, src_ref, dst_ref, device):
        k = number(name)
        return pltpu.make_async_remote_copy(
            src_ref=src_ref, dst_ref=dst_ref, send_sem=send_sem.at[k], recv_sem=recv_sem.at[k],
            device_id=device, device_id_type=MESH,
        )

    sent = []

    def send(name, src_ref, dst_ref, device):
        copy = remote(name, src_ref, dst_ref, device)
        copy.start()
        sent.append(copy)

    def arrived(name, ref):
        remote(name, ref, ref, {"narrow": block[1]}).wait_recv()

    loads = {}

    def load(name, src_ref, dst_ref):
        copy = pltpu.make_async_copy(src_ref, dst_ref, load_sem.at[len(loads)])
        loads[name] = copy
        copy.start()

    stores = []

    def store(src_ref, dst_ref):
        copy = pltpu.make_async_copy(src_ref, dst_ref, store_sem.at[len(stores)])
        stores.append(copy)
        copy.start()

    def rows(m):
        return pl.ds(place[m] * R, R)

    def natural(j):
        return pl.ds(pl.multiple_of(j * R, R), R)

    def column(j):
        return pl.ds(pl.multiple_of(j * CC, CC), CC)

    def shard(j):
        return pl.ds(pl.multiple_of(j * K, K), K)

    def half(h):
        return pl.ds(h * HD, HD)

    load("up", up_hbm, uw)
    load("down", down_hbm, dw)
    load("g", g_hbm, g.at[rows(0)])
    for m in (3, 1):
        load(("tok", m), tok_hbm.at[natural(block[m])], tok.at[rows(m)])
    for q in range(4):
        load(("w", q), w_hbm.at[pl.ds(q * (D // 4), D // 4)], w.at[pl.ds(q * (D // 4), D // 4)])
    for m in (2, 0):
        load(("tok", m), tok_hbm.at[natural(block[m])], tok.at[rows(m)])
    for m in order:
        load(("idx", m), idx_hbm.at[:, natural(block[m])], idx.at[:, rows(m)])
    for name, src_ref, dst_ref in (
        ("dm1", dm1_hbm, dm1), ("dm2", dm2_hbm, dm2), ("um1", um1_hbm, um1), ("um2", um2_hbm, um2),
        ("rates", rates_hbm, rates_ref),
    ):
        load(name, src_ref, dst_ref)

    barrier = pltpu.get_barrier_semaphore()
    for m in (1, 2, 3):
        pl.semaphore_signal(barrier, inc=1, device_id={"narrow": block[m]}, device_id_type=MESH)
    for d in range(1, wide):
        pl.semaphore_signal(
            barrier, inc=1, device_id={"wide": lax.rem(z + d, wide)}, device_id_type=MESH
        )
    loads["up"].wait()
    upf[shard(z), column(me)] = uw[...].astype(jnp.bfloat16)
    loads["down"].wait()
    downf[shard(z), :] = dw[...].astype(jnp.bfloat16)
    loads["g"].wait()
    pl.semaphore_wait(barrier, 3 + wide - 1)

    for d in range(1, wide):
        mine = upf.at[shard(z), column(me)]
        send(("up", d), mine, mine, {"wide": lax.rem(z + d, wide)})

    chain_sent = []

    def guarded_send(cond, name, src_ref, dst_ref, device):
        copy = remote(name, src_ref, dst_ref, device)
        pl.when(cond)(copy.start)
        chain_sent.append((cond, copy))

    def down_step(s):
        for h in range(HALVES):
            if s >= 1:
                @pl.when(z - s >= 0)
                def _():
                    arrived(("down_r", s - 1, h), downf.at[shard(z - s), half(h)])

            if s <= wide - 2:
                part = downf.at[shard(jnp.maximum(z - s, 0)), half(h)]
                guarded_send(
                    (z - s >= 0) & (z < wide - 1), ("down_r", s, h), part, part,
                    {"wide": jnp.minimum(z + 1, wide - 1)},
                )
            if s >= 1:
                @pl.when(z + s <= wide - 1)
                def _():
                    arrived(("down_l", s - 1, h), downf.at[shard(z + s), half(h)])

            if s <= wide - 2:
                part = downf.at[shard(jnp.minimum(z + s, wide - 1)), half(h)]
                guarded_send(
                    (z + s <= wide - 1) & (z > 0), ("down_l", s, h), part, part,
                    {"wide": jnp.maximum(z - 1, 0)},
                )

    down_step(0)

    for m, core in ((2, c), (3, co)):
        part = column(xo * 2 + core)
        send(("g", m, 0), g.at[rows(0), part], g.at[rows(m), part], {"narrow": block[m]})
    send("g_sib", g.at[rows(0)], g.at[rows(1)], {"narrow": block[1]})
    for m, core in ((2, c), (3, co)):
        part = column(x * 2 + core)
        send(("g", m, 1), g.at[rows(0), part], g.at[rows(m), part], {"narrow": block[m]})

    for m in order:
        loads["idx", m].wait()
    adapter = lax.broadcasted_iota(jnp.int32, (A, T), 0) // ADAPTER_RANK

    def member():
        return adapter == jnp.broadcast_to(idx[...], (A, T))

    def pack(full):
        chosen = jnp.where(member(), full, 0.0)
        total = chosen[0:ADAPTER_RANK]
        for a in range(1, members):
            total = total + chosen[a * ADAPTER_RANK : (a + 1) * ADAPTER_RANK]
        return total

    def spread_out(packed):
        return jnp.where(member(), jnp.concatenate([packed] * members, axis=0), 0.0)

    def exchange(name, packed, out, box):
        low = packed.astype(jnp.bfloat16)
        for m in order:
            out[:, natural(block[m])] = low[:, place[m] * R : (place[m] + 1) * R]
        for m in (2, 3, 1):
            send((name, m), out, box.at[m - 1], {"narrow": block[m]})

    def total_of(name, packed, box, nat):
        for m in (1, 2, 3):
            arrived((name, m), box.at[m - 1])
        nat[...] = box[0].astype(jnp.float32) + box[1].astype(jnp.float32) + box[2].astype(jnp.float32)
        return packed + jnp.concatenate([nat[:, natural(block[m])] for m in order], axis=1)

    for d in range(1, wide):
        arrived(("up", d), upf.at[shard(lax.rem(z - d + wide, wide)), column(me)])
    arrived("g_sib", g.at[rows(1)])
    for m in (2, 3):
        arrived(("g", m, 0), g.at[rows(m), column(me)])
    back_part = pack(dot_nt(upf[:, column(me)], g[:, column(me)]))
    exchange("back", back_part, bsend, brecv)
    for m, to in ((2, 3), (3, 2)):
        send(("g_fwd", m, 0), g.at[rows(m), column(me)], g.at[rows(to), column(me)], {"narrow": block[1]})
    for m in (2, 1):
        mine = upf.at[:, column(me)]
        send(("up_x", m), mine, mine, {"narrow": block[m]})

    down_step(1)

    loads["tok", 3].wait()
    loads["tok", 1].wait()
    for q in range(4):
        loads["w", q].wait()
    for q in range(4):
        cols = pl.ds(q * CC, CC)
        psend[:, cols] = dot_nn(tok[0 : 2 * R, :], w[:, cols]).astype(jnp.bfloat16)
    send("p", psend, precv, {"narrow": block[1]})

    loads["tok", 2].wait()
    loads["tok", 0].wait()

    back = 2.0 * total_of("back", back_part, brecv, bnat)
    back_wide_t = spread_out(back)
    back_low = back_wide_t.astype(jnp.bfloat16)
    for h in range(HALVES):
        dpart[:, half(h)] = dot_nn(back_low, tok[:, half(h)])

    rs_sent = []

    def rs_step(k):
        for right in (True, False):
            j = wide - 1 - k if right else k
            box = rs_left if right else rs_right
            name = "rs_r" if right else "rs_l"
            ahead = (j > z) if right else (j < z)
            follows = (z > 0) if right else (z < wide - 1)
            target = jnp.minimum(z + 1, wide - 1) if right else jnp.maximum(z - 1, 0)
            for h in range(HALVES):
                own = dpart.at[pl.ds(j * K, K), half(h)]
                stage = rs_stage.at[j, :, half(h)]
                landing = box.at[j, :, half(h)]

                @pl.when(ahead & follows)
                def _():
                    arrived((name, k, h), landing)
                    stage[...] = (own[...] + landing[...].astype(jnp.float32)).astype(jnp.bfloat16)

                @pl.when(ahead & jnp.logical_not(follows))
                def _():
                    stage[...] = own[...].astype(jnp.bfloat16)

                copy = remote((name, k, h), stage, landing, {"wide": target})
                pl.when(ahead)(copy.start)
                rs_sent.append((ahead, copy))

    rs_step(0)

    for s in range(2, wide - 1):
        down_step(s)

    for q in range(4):
        cols = pl.ds(q * CC, CC)
        pacc[:, cols] = dot_nn(tok[2 * R :, :], w[:, cols])
    arrived("p", precv)
    xsend[...] = (pacc[0:R] + precv[0:R].astype(jnp.float32)).astype(jnp.bfloat16)
    send("px", xsend, xrecv, {"narrow": block[2]})

    if wide > 2:
        down_step(wide - 1)

    for m, to in ((2, 3), (3, 2)):
        part = column(xo * 2 + c)
        arrived(("g", m, 1), g.at[rows(m), part])
        send(("g_fwd", m, 1), g.at[rows(m), part], g.at[rows(to), part], {"narrow": block[1]})
    arrived(("up_x", 2), upf.at[:, column(block[2])])
    part = upf.at[:, column(block[2])]
    send("up_fwd", part, part, {"narrow": block[1]})

    code_part = pack(dot_nt(tok[...], downf[...]).T)
    exchange("code", code_part, csend, crecv)
    if wide > 2:
        rs_step(1)

    for m in (2, 3):
        arrived(("g_fwd", 5 - m, 0), g.at[rows(m), column(block[1])])
        arrived(("g_fwd", 5 - m, 1), g.at[rows(m), column(block[3])])
    back_rows = back_wide_t.T.astype(jnp.bfloat16)

    def grad_tokens(part, parts):
        width = D // parts
        span = pl.ds(part * width, width)
        gt[:, span] = (dot_nt(g[...], w[span, :]) + dot_nn(back_rows, downf[:, span])).astype(jnp.bfloat16)
        for m in order:
            store(gt.at[rows(m), span], gt_out.at[natural(block[m]), span])

    grad_tokens(0, 4)

    code = total_of("code", code_part, crecv, cnat)
    code_wide_t = spread_out(code)
    code_low = code_wide_t.astype(jnp.bfloat16)
    gu_stage[...] = (2.0 * dot_nn(code_low, g[:, column(me)])).astype(jnp.bfloat16)
    for d in range(1, wide):
        to = lax.rem(z + d, wide)
        send(("gu", d), gu_stage.at[shard(to)], gu_recv.at[d], {"wide": to})

    for k in range(2, wide - 1):
        rs_step(k)
    grad_tokens(1, 4)
    grad_tokens(2, 4)
    grad_tokens(3, 4)

    arrived(("up_x", 1), upf.at[:, column(block[1])])
    arrived("up_fwd", upf.at[:, column(block[3])])
    code_rows = code_wide_t[:, place[0] * R : (place[0] + 1) * R].T.astype(jnp.bfloat16)
    delta = dot_nn(code_rows, upf[...])
    arrived("px", xrecv)
    vals[...] = (
        pacc[R : 2 * R] + precv[R : 2 * R].astype(jnp.float32) + xrecv[...].astype(jnp.float32) + 2.0 * delta
    ).astype(jnp.bfloat16)
    store(vals, val_out)

    loads["rates"].wait()
    owner = lax.broadcasted_iota(jnp.int32, (K, 1), 0) // ADAPTER_RANK
    rate = jnp.zeros((K, 1), jnp.float32)
    for a in range(K // ADAPTER_RANK):
        rate = jnp.where(owner == a, rates_ref[a], rate)

    grad_up = gu_stage[shard(z), :].astype(jnp.float32)
    for d in range(1, wide):
        arrived(("gu", d), gu_recv.at[d])
        grad_up = grad_up + gu_recv[d].astype(jnp.float32)
    loads["um1"].wait()
    loads["um2"].wait()
    uw[...], um1[...], um2[...] = apply_adam_moments(uw[...], um1[...], um2[...], grad_up, rate)
    store(uw, uw_out)
    store(um1, um1_out)
    store(um2, um2_out)

    loads["dm1"].wait()
    loads["dm2"].wait()
    for h in range(HALVES):
        cols = half(h)
        for j in range(wide):
            if j > 0:
                @pl.when(z == j)
                def _():
                    landing = rs_left.at[j, :, cols]
                    arrived(("rs_r", wide - 1 - j, h), landing)
                    own = dpart.at[pl.ds(j * K, K), cols]
                    own[...] = own[...] + landing[...].astype(jnp.float32)

            if j < wide - 1:
                @pl.when(z == j)
                def _():
                    landing = rs_right.at[j, :, cols]
                    arrived(("rs_l", j, h), landing)
                    own = dpart.at[pl.ds(j * K, K), cols]
                    own[...] = own[...] + landing[...].astype(jnp.float32)

        grad_down = dpart[shard(z), cols]
        dw[:, cols], dm1[:, cols], dm2[:, cols] = apply_adam_moments(
            dw[:, cols], dm1[:, cols], dm2[:, cols], grad_down, rate
        )
        store(dw.at[:, cols], dw_out.at[:, cols])
        store(dm1.at[:, cols], dm1_out.at[:, cols])
        store(dm2.at[:, cols], dm2_out.at[:, cols])

    for copy in sent:
        copy.wait_send()
    for cond, copy in chain_sent + rs_sent:
        pl.when(cond)(copy.wait_send)
    for copy in stores:
        copy.wait()


def write_kernel(*refs):
    held, load_sem, store_sem = refs[16:24], refs[24], refs[25]
    parts = 4
    pieces = []
    for k in (1, 0, 2, 3, 4, 5, 6, 7):
        cuts = parts if k == 1 else 1
        size = refs[k].shape[0] // cuts
        for part in range(cuts):
            rows, n = pl.ds(part * size, size), len(pieces)
            pieces.append((
                pltpu.make_async_copy(refs[k].at[rows], held[k].at[rows], load_sem.at[n]),
                pltpu.make_async_copy(held[k].at[rows], refs[8 + k].at[rows], store_sem.at[n]),
            ))
    for load, _ in pieces:
        load.start()
    for load, store in pieces:
        load.wait()
        store.start()
    for _, store in pieces:
        store.wait()


def fused_shards(
    tokens,
    frozen_value_weight,
    token_adapter_index,
    adapter_down_weight,
    adapter_up_weight,
    down_moment_first,
    down_moment_second,
    up_moment_first,
    up_moment_second,
    rates,
    value_output_gradient,
):
    wide = lax.axis_size("wide")
    T, D = tokens.shape
    C = frozen_value_weight.shape[1]
    R, CC = T // 4, C // 4
    K = adapter_down_weight.shape[1]
    A = K * wide
    f32, low = jnp.float32, jnp.bfloat16
    shape = jax.ShapeDtypeStruct
    remotes = 2 * (wide - 1) + 16 + 4 * HALVES * (wide - 1) + 8
    any_spec = pl.BlockSpec(memory_space=pl.ANY)
    hbm_spec = pl.BlockSpec(memory_space=pltpu.HBM)
    outs = pl.pallas_call(
        functools.partial(fused_kernel, wide),
        out_shape=(
            shape((R, C), low), shape((T, D), low),
            shape((K, D), f32), shape((K, D), f32), shape((K, D), f32),
            shape((K, CC), f32), shape((K, CC), f32), shape((K, CC), f32),
        ),
        in_specs=[hbm_spec] * 11,
        out_specs=(any_spec,) * 8,
        scratch_shapes=[
            pltpu.VMEM((T, D), low), pltpu.VMEM((D, C), low), pltpu.VMEM((1, T), jnp.int32),
            pltpu.VMEM((T, C), low), pltpu.VMEM((A, C), low), pltpu.VMEM((A, D), low),
            pltpu.VMEM((K, D), f32), pltpu.VMEM((K, D), f32), pltpu.VMEM((K, D), f32),
            pltpu.VMEM((K, CC), f32), pltpu.VMEM((K, CC), f32), pltpu.VMEM((K, CC), f32),
            pltpu.VMEM((2 * R, C), low), pltpu.VMEM((2 * R, C), low), pltpu.VMEM((2 * R, C), f32),
            pltpu.VMEM((R, C), low), pltpu.VMEM((R, C), low),
            pltpu.VMEM((ADAPTER_RANK, T), low), pltpu.VMEM((3, ADAPTER_RANK, T), low),
            pltpu.VMEM((ADAPTER_RANK, T), f32),
            pltpu.VMEM((ADAPTER_RANK, T), low), pltpu.VMEM((3, ADAPTER_RANK, T), low),
            pltpu.VMEM((ADAPTER_RANK, T), f32),
            pltpu.VMEM((A, D), f32), pltpu.VMEM((wide, K, D), low),
            pltpu.VMEM((wide, K, D), low), pltpu.VMEM((wide, K, D), low),
            pltpu.VMEM((8, 128), f32), pltpu.VMEM((T, D), low),
            pltpu.VMEM((A, CC), low), pltpu.VMEM((wide, K, CC), low), pltpu.VMEM((R, C), low),
            pltpu.SMEM(rates.shape, f32),
            pltpu.SemaphoreType.DMA((20,)), pltpu.SemaphoreType.DMA((16 + 4 + 3 * HALVES,)),
            pltpu.SemaphoreType.DMA((remotes,)), pltpu.SemaphoreType.DMA((remotes,)),
        ],
        compiler_params=pltpu.CompilerParams(
            collective_id=0, has_side_effects=True, vmem_limit_bytes=64 * 1024 * 1024 - 65536
        ),
        cost_estimate=pl.CostEstimate(
            flops=2 * (2 * T * D * C + 3 * T * D * A), bytes_accessed=12 * 1024 * 1024, transcendentals=0
        ),
    )(
        tokens, frozen_value_weight, token_adapter_index.reshape(1, T),
        adapter_down_weight.T, adapter_up_weight,
        down_moment_first.T, down_moment_second.T, up_moment_first, up_moment_second,
        rates, value_output_gradient,
    )
    values, grad_tokens, dw, dm1, dm2, uw, um1, um2 = pl.pallas_call(
        write_kernel,
        out_shape=tuple(shape(a.shape, a.dtype) for a in outs),
        in_specs=[any_spec] * 8,
        out_specs=(hbm_spec,) * 8,
        scratch_shapes=[pltpu.VMEM(a.shape, a.dtype) for a in outs]
        + [pltpu.SemaphoreType.DMA((11,)), pltpu.SemaphoreType.DMA((11,))],
    )(*outs)
    return (values, grad_tokens, dw.T, dm1.T, dm2.T, uw, um1, um2)


def solution(mesh):
    return jax.shard_map(
        fused_shards if mesh.shape["narrow"] == 4 and mesh.shape["wide"] > 1 else shards,
        mesh=mesh,
        in_specs=(
            P(("grid", "wide"), "narrow"),
            P("narrow", None),
            P(("grid", "wide"), None),
            P(("grid", "narrow"), "wide"),
            P(("grid", "wide"), "narrow"),
            P(("grid", "narrow"), "wide"),
            P(("grid", "narrow"), "wide"),
            P(("grid", "wide"), "narrow"),
            P(("grid", "wide"), "narrow"),
            P(("grid", "wide")),
            P(("grid", "wide", "narrow"), None),
        ),
        out_specs=(
            P(("grid", "wide", "narrow"), None),
            P(("grid", "wide"), "narrow"),
            P(("grid", "narrow"), "wide"),
            P(("grid", "narrow"), "wide"),
            P(("grid", "narrow"), "wide"),
            P(("grid", "wide"), "narrow"),
            P(("grid", "wide"), "narrow"),
            P(("grid", "wide"), "narrow"),
        ),
        check_vma=False,
    )
```
